512 devices in a mesh: grp: 8 (over x, z_lo), fsdp: 8 (over y), seq: 8 (over z_hi, core).
Axes of the slice: x: 4, y: 8, z: 8 (z_hi: 4, z_lo: 2; z = z_hi * 2 + z_lo), core: 2. Of those that a mesh axis runs over, the one named last changes fastest.
Arguments:
- img_qkv: bfloat16 [64, 1024, 3, 2048], P(('grp', 'fsdp'), 'seq'), may hold values from -15 to 15
- txt_kv: bfloat16 [64, 256, 2, 2048], P(None, ('grp', 'fsdp'), None, 'seq'), may hold values from -15 to 15
- cot_img: bfloat16 [64, 1024, 2048], P(('grp', 'fsdp'), 'seq'), may hold values from -6 to 6
- timesteps: int32 [64], P(('grp', 'fsdp')), may hold values from 0 to 999
- lengths: int32 [64], P(('grp', 'fsdp')), may hold values from 1 to 256
- gate_w: bfloat16 [256, 2048], P(None, 'seq'), may hold values from -0.375 to 0.375
- gain_q: float32 [128], replicated, may hold values from 0.1 to 1.9
- gain_k: float32 [128], replicated, may hold values from 0.1 to 1.9
- gain_t: float32 [128], replicated, may hold values from 0.1 to 1.9
Outputs:
- out_img: bfloat16 [64, 1024, 2048], P(('grp', 'fsdp'), 'seq')
- d_img_qkv: bfloat16 [64, 1024, 3, 2048], P(('grp', 'fsdp'), 'seq')
- d_txt_kv: bfloat16 [64, 256, 2, 2048], P(None, ('grp', 'fsdp'), None, 'seq')
The draws below stay inside these ranges and needn't reach their ends.
All inputs are finite; a program needn't handle non-finite values.
Results may differ from the reference program's by a relative error of at most 0.0085.
Values may be sent and summed in bfloat16 or wider, within the bound.
No kernel may reach another device: no remote copies, remote signals or barrier semaphores. Data moves between devices by JAX's collectives and lax.ppermute only.
A program may use at most 64 MiB of HBM per device.

```python
import math
import jax
import jax.numpy as jnp
from jax import lax

D = 2048
HEADS = 16
HS = 128
P_SIZE = 256
FREQ = 256
NT = 1000
L = 1024
B = 64


def scaled_draw(key, lead_shape, head_count, head_size):
    key_base, key_rows, key_cols = jax.random.split(key, 3)
    full_shape = lead_shape + (head_count, head_size)
    base_vals = jax.random.truncated_normal(key_base, -3.0, 3.0, full_shape, jnp.float32)
    row_scale = jnp.exp(jax.random.uniform(key_rows, lead_shape + (head_count, 1), jnp.float32, math.log(0.3), math.log(3.0)))
    col_scale = jnp.exp(jax.random.uniform(key_cols, (head_count, head_size), jnp.float32, -0.5, 0.5))
    values_out = base_vals * row_scale * col_scale
    return values_out.reshape(lead_shape + (head_count * head_size,)).astype(jnp.bfloat16)


def draw_img_qkv(key, part):
    return scaled_draw(jax.random.fold_in(key, 11), (B, L, 3), HEADS, D // HEADS)


def draw_txt_kv(key, part):
    return scaled_draw(jax.random.fold_in(key, 23), (B, P_SIZE, 2), HEADS, D // HEADS)


def place_ends(drawn, stream_key, low, largest):
    spot = [jax.random.randint(jax.random.fold_in(stream_key, axis), (), 0, length) for axis, length in enumerate(drawn.shape)]
    longest = drawn.shape.index(max(drawn.shape))
    next_to = spot[:longest] + [(spot[longest] + 1) % drawn.shape[longest]] + spot[longest + 1:]
    return drawn.at[tuple(spot)].set(low).at[tuple(next_to)].set(largest)


def block_levels(stream_key, dims, shards, low, largest):
    gain = 1.0
    for dim, shards_of in shards:
        heights = jax.random.uniform(jax.random.fold_in(jax.random.fold_in(stream_key, 6), dim), (shards_of,), jnp.float32, low / len(shards), largest / len(shards))
        gain = gain * jnp.repeat(jnp.exp(heights), dims[dim] // shards_of).reshape((-1,) + (1,) * (len(dims) - 1 - dim))
    return gain


def normal_values(key, shape, spread, limit, cuts=(), kind=jnp.bfloat16):
    values = spread * jax.random.normal(key, shape, jnp.float32)
    if cuts:
        values = values * block_levels(key, shape, cuts, -0.22, 0.18)
    return jnp.clip(values, -limit, limit).astype(kind)


def setup_inputs(seed: int = 0) -> dict:
    streams_of = jax.random.split(jax.random.key(seed), 10)
    return {
        "img_qkv": draw_img_qkv(jax.random.fold_in(streams_of[9], 71), 0),
        "txt_kv": draw_txt_kv(jax.random.fold_in(streams_of[9], 71), 0),
        "cot_img": normal_values(streams_of[2], (B, L, D), 1.0, 6.0, ((0, 64), (1, 8))),
        "timesteps": place_ends(jax.random.randint(streams_of[3], (B,), 0, NT), jax.random.fold_in(streams_of[3], 1), 0, NT - 1).astype(jnp.int32),
        "lengths": place_ends(jax.random.randint(streams_of[4], (B,), 1, P_SIZE + 1), jax.random.fold_in(streams_of[4], 1), 1, P_SIZE).astype(jnp.int32),
        "gate_w": normal_values(streams_of[5], (FREQ, D), FREQ ** -0.5, 0.375, ((1, 8),)),
        "gain_q": jnp.clip(1.0 + 0.18 * jax.random.normal(streams_of[6], (HS,), jnp.float32), 0.1, 1.9),
        "gain_k": jnp.clip(1.0 + 0.18 * jax.random.normal(streams_of[7], (HS,), jnp.float32), 0.1, 1.9),
        "gain_t": jnp.clip(1.0 + 0.18 * jax.random.normal(streams_of[8], (HS,), jnp.float32), 0.1, 1.9),
    }


norm_eps = 1e-06

def normed(vector, scale_gain):
    vector_wide = vector.astype(jnp.float32)
    inverse_rms = lax.rsqrt(lax.optimization_barrier(jnp.mean(vector_wide * vector_wide, axis=-1, keepdims=True)) + norm_eps)
    return (vector_wide * inverse_rms * scale_gain).astype(jnp.bfloat16)

def norm_back(vector, scale_gain, upstream_grad):
    vector_wide = vector.astype(jnp.float32)
    inverse_rms = lax.rsqrt(lax.optimization_barrier(jnp.mean(vector_wide * vector_wide, axis=-1, keepdims=True)) + norm_eps)
    weighted = upstream_grad * scale_gain
    cubed = inverse_rms * inverse_rms * inverse_rms
    along = lax.optimization_barrier(jnp.mean(vector_wide * weighted, axis=-1, keepdims=True))
    return (weighted * inverse_rms - vector_wide * cubed * along).astype(jnp.bfloat16)

def embedding(stamps, half_freq):
    frequency = jnp.exp(-math.log(10000.0) * jnp.arange(half_freq, dtype=jnp.float32) / half_freq)
    angles = stamps.astype(jnp.float32)[..., None] * frequency
    return jnp.concatenate([jnp.cos(angles), jnp.sin(angles)], axis=-1)

def attend(queries, keys_img, values_img, keys_txt, values_txt, cotangent, gate_heads, prompt_len, gain_q, gain_k, gain_t, block_width, block_count):
    query_rows, head_count, head_size = queries.shape
    prompt_rows = keys_txt.shape[0]
    score_scale = 1.0 / math.sqrt(head_size)
    query_norm = normed(queries, gain_q)
    key_norm = normed(keys_img, gain_k)
    text_norm = normed(keys_txt, gain_t)
    exp_image = jnp.exp(jnp.einsum('qhd,khd->hqk', query_norm, key_norm, preferred_element_type=jnp.float32) * score_scale)

    def text_exp(block_index):
        first_row = block_index.astype(jnp.int32) * block_width
        key_block = lax.dynamic_slice_in_dim(text_norm, first_row, block_width, 0)
        positions = first_row + jnp.arange(block_width, dtype=jnp.int32)
        raw_exp = jnp.exp(jnp.einsum('qhd,khd->hqk', query_norm, key_block, preferred_element_type=jnp.float32) * score_scale)
        live = (positions < prompt_len)[None, None, :]
        return (jnp.where(live, raw_exp, 0.0), first_row, key_block)

    def add_total(block_index, running):
        return running + lax.optimization_barrier(jnp.sum(text_exp(block_index)[0], axis=-1))
    denom_sum = lax.optimization_barrier(jnp.sum(exp_image, axis=-1)) + lax.fori_loop(0, block_count, add_total, jnp.zeros((head_count, query_rows), jnp.float32))
    prob_image = exp_image / denom_sum[:, :, None]
    weight_image = prob_image.astype(jnp.bfloat16)

    def add_values(block_index, running):
        exp_text, first_row, key_block = text_exp(block_index)
        value_block = lax.dynamic_slice_in_dim(values_txt, first_row, block_width, 0)
        weight_text = (exp_text / denom_sum[:, :, None]).astype(jnp.bfloat16)
        return running + jnp.einsum('hqk,khd->qhd', weight_text, value_block, preferred_element_type=jnp.float32)
    attention = jnp.einsum('hqk,khd->qhd', weight_image, values_img, preferred_element_type=jnp.float32) + lax.fori_loop(0, block_count, add_values, jnp.zeros((query_rows, head_count, head_size), jnp.float32))
    gated_out = (attention * gate_heads).astype(jnp.bfloat16)
    grad_attention = (cotangent.astype(jnp.float32) * gate_heads).astype(jnp.bfloat16)
    row_delta = lax.optimization_barrier(jnp.sum(grad_attention.astype(jnp.float32) * attention, axis=-1)).T
    grad_value = jnp.einsum('hqk,qhd->khd', weight_image, grad_attention, preferred_element_type=jnp.float32).astype(jnp.bfloat16)
    grad_prob = jnp.einsum('qhd,khd->hqk', grad_attention, values_img, preferred_element_type=jnp.float32)
    grad_score = (prob_image * (grad_prob - row_delta[:, :, None])).astype(jnp.bfloat16)
    grad_qnorm = jnp.einsum('hqk,khd->qhd', grad_score, key_norm, preferred_element_type=jnp.float32)
    grad_knorm = jnp.einsum('hqk,qhd->khd', grad_score, query_norm, preferred_element_type=jnp.float32) * score_scale

    def text_back(block_index, loop_state):
        running, grad_tkeys, grad_tvalues = loop_state
        exp_text, first_row, key_block = text_exp(block_index)
        value_block = lax.dynamic_slice_in_dim(values_txt, first_row, block_width, 0)
        raw_block = lax.dynamic_slice_in_dim(keys_txt, first_row, block_width, 0)
        prob_text = exp_text / denom_sum[:, :, None]
        weight_text = prob_text.astype(jnp.bfloat16)
        grad_vblock = jnp.einsum('hqk,qhd->khd', weight_text, grad_attention, preferred_element_type=jnp.float32).astype(jnp.bfloat16)
        grad_pblock = jnp.einsum('qhd,khd->hqk', grad_attention, value_block, preferred_element_type=jnp.float32)
        grad_sblock = (prob_text * (grad_pblock - row_delta[:, :, None])).astype(jnp.bfloat16)
        running = running + jnp.einsum('hqk,khd->qhd', grad_sblock, key_block, preferred_element_type=jnp.float32)
        grad_kblock = norm_back(raw_block, gain_t, jnp.einsum('hqk,qhd->khd', grad_sblock, query_norm, preferred_element_type=jnp.float32) * score_scale)
        grad_tkeys = lax.dynamic_update_slice_in_dim(grad_tkeys, grad_kblock, first_row, 0)
        grad_tvalues = lax.dynamic_update_slice_in_dim(grad_tvalues, grad_vblock, first_row, 0)
        return (running, grad_tkeys, grad_tvalues)
    zero_prompt = jnp.zeros((prompt_rows, head_count, head_size), jnp.bfloat16)
    running, grad_tkey, grad_tvalue = lax.fori_loop(0, block_count, text_back, (jnp.zeros((query_rows, head_count, head_size), jnp.float32), zero_prompt, zero_prompt))
    grad_query = norm_back(queries, gain_q, (grad_qnorm + running) * score_scale)
    grad_key = norm_back(keys_img, gain_k, grad_knorm)
    return (gated_out, grad_query, grad_key, grad_value, grad_tkey, grad_tvalue)

def reference(img_qkv, txt_kv, cot_img, timesteps, lengths, gate_w, gain_q, gain_k, gain_t):
    head_size = D // HEADS
    embedded = embedding(timesteps, FREQ // 2)
    gate_all = jnp.dot(embedded, gate_w.astype(jnp.float32), precision=lax.Precision.HIGHEST)

    def one_sample(sample_items):
        image_part, prompt_part, cotangent, gate_row, prompt_len = sample_items
        image_part = image_part.reshape(L, 3, HEADS, head_size)
        prompt_part = prompt_part.reshape(P_SIZE, 2, HEADS, head_size)
        results = attend(image_part[:, 0], image_part[:, 1], image_part[:, 2], prompt_part[:, 0], prompt_part[:, 1], cotangent.reshape(L, HEADS, head_size), gate_row.reshape(HEADS, head_size), prompt_len, gain_q, gain_k, gain_t, P_SIZE, 1)
        gated_out, grad_query, grad_key, grad_value, grad_tkey, grad_tvalue = results
        image_grads = jnp.stack([grad_query, grad_key, grad_value], axis=1).reshape(L, 3, D)
        prompt_grads = jnp.stack([grad_tkey, grad_tvalue], axis=1).reshape(P_SIZE, 2, D)
        return (gated_out.reshape(L, D), image_grads, prompt_grads)
    out_img, d_img_qkv, d_txt_kv = lax.map(one_sample, (img_qkv, txt_kv, cot_img, gate_all, lengths))
    return (out_img, d_img_qkv, d_txt_kv)
```

```python
import math

import jax
import jax.numpy as jnp
from jax import lax
from jax.experimental import pallas as pl
from jax.experimental.pallas import tpu as pltpu
from jax.sharding import PartitionSpec as P

D = 2048
HEADS = 16
HS = D // HEADS
EPS = 1e-06
SCALE = 1.0 / math.sqrt(HS)
EXP2_SCALE = SCALE * math.log2(math.e)
CHIPS = 4
SEQ = 2 * CHIPS
OFFSETS = ((2, 0), (2, 1), (1, 0), (3, 0), (1, 1), (3, 1), (0, 1), (0, 0))
ROWS = 128
WIDTH = 256
HPD = WIDTH // HS
L = SEQ * ROWS
PROMPT = 256
KEYS = L + PROMPT
BLOCK = 2
QROWS = BLOCK * ROWS


def embedding(stamps, half_freq):
    frequency = jnp.exp(-math.log(10000.0) * jnp.arange(half_freq, dtype=jnp.float32) / half_freq)
    angles = stamps.astype(jnp.float32)[..., None] * frequency
    return jnp.concatenate([jnp.cos(angles), jnp.sin(angles)], axis=-1)


def normed(x, gain):
    r = lax.rsqrt(jnp.mean(x * x, axis=-1, keepdims=True) + EPS)
    return (x * r * gain).astype(jnp.bfloat16)


def norm_back(x, gain, upstream):
    r = lax.rsqrt(jnp.mean(x * x, axis=-1, keepdims=True) + EPS)
    weighted = upstream * gain
    along = jnp.mean(x * weighted, axis=-1, keepdims=True)
    return (weighted * r - x * (r * r * r * along)).astype(jnp.bfloat16)


def dot(a, b, dims):
    return lax.dot_general(a, b, (dims, ((), ())), preferred_element_type=jnp.float32)


NT = ((1,), (1,))
NN = ((1,), (0,))


def position():
    me = lax.axis_index("seq")
    return me // 2, me % 2


def partner(i, c, offset):
    dz, dc = offset
    return ((i + dz) % CHIPS) * 2 + (c + dc) % 2


def pack_kernel(place, img, cot, *outs):
    for offset, out in zip(OFFSETS, outs):
        d = partner(place[0], place[1], offset)
        columns = pl.ds(pl.multiple_of(d * WIDTH, WIDTH), WIDTH)
        out[:3] = img[:, :, columns]
        out[3] = cot[:, columns]


def unpack_kernel(place, *refs):
    packed, (out, grads) = refs[:SEQ], refs[SEQ:]
    for offset, part in zip(OFFSETS, packed):
        d = partner(place[0], place[1], offset)
        columns = pl.ds(pl.multiple_of(d * WIDTH, WIDTH), WIDTH)
        out[:, columns] = part[0]
        grads[:, :, columns] = part[1:]


def attend_kernel(length, txt, gate, gain_q, gain_k, gain_t, *refs):
    received, sent, d_txt = refs[:SEQ], refs[SEQ : 2 * SEQ], refs[2 * SEQ]
    rin, rout, kn, kt, ve, vt, dk, dv, sems = refs[2 * SEQ + 1 :]
    copies = [pltpu.make_async_copy(r, rin.at[s], sems.at[s]) for s, r in enumerate(received)]
    for copy in copies:
        copy.start()
    for copy in copies:
        copy.wait()
    gq, gk, gt = gain_q[...], gain_k[...], gain_t[...]
    live = lax.broadcasted_iota(jnp.int32, (PROMPT, HS), 0) < length[0]
    lane = lax.broadcasted_iota(jnp.int32, (QROWS, HS), 1)
    for h in range(HPD):
        columns = pl.ds(h * HS, HS)
        gate_h = gate[:, columns]
        k_img = rin[:, 1, :, columns].reshape(L, HS).astype(jnp.float32)
        kn[:L] = normed(k_img, gk)
        kn[L:] = normed(txt[:, 0, columns].astype(jnp.float32), gt)
        ve[:L, :HS] = rin[:, 2, :, columns].reshape(L, HS)
        ve[:L, HS:] = jnp.ones((L, HS), jnp.bfloat16)
        ve[L:, :HS] = jnp.where(live, txt[:, 1, columns].astype(jnp.float32), 0.0).astype(jnp.bfloat16)
        ve[L:, HS:] = jnp.where(live, 1.0, 0.0).astype(jnp.bfloat16)
        kt[...] = kn[...].T
        vt[...] = ve[...].T
        dk[...] = jnp.zeros_like(dk)
        dv[...] = jnp.zeros_like(dv)

        def step(j, carry):
            rows = pl.ds(j * BLOCK, BLOCK)
            q = rin[rows, 0, :, columns].reshape(QROWS, HS).astype(jnp.float32)
            cot = rin[rows, 3, :, columns].reshape(QROWS, HS).astype(jnp.float32)
            qn = normed(q, gq)
            e = jnp.exp2(dot(kn[...], qn, NT) * EXP2_SCALE)
            eb = e.astype(jnp.bfloat16)
            sums = dot(vt[...], eb, NN).T
            rz = 1.0 / sums[:, HS:]
            attn = sums[:, :HS] * rz
            rout[rows, 0, :, columns] = (attn * gate_h).astype(jnp.bfloat16).reshape(BLOCK, ROWS, HS)
            g = (cot * gate_h * rz).astype(jnp.bfloat16)
            delta = -jnp.sum(g.astype(jnp.float32) * attn, axis=-1, keepdims=True)
            hi = delta.astype(jnp.bfloat16).astype(jnp.float32)
            mid = (delta - hi).astype(jnp.bfloat16).astype(jnp.float32)
            low = delta - hi - mid
            tail = jnp.where(lane == 0, hi, jnp.where(lane == 1, mid, jnp.where(lane == 2, low, 0.0)))
            ge = jnp.concatenate([g, tail.astype(jnp.bfloat16)], axis=1)
            ds = (e * dot(ve[...], ge, NT)).astype(jnp.bfloat16)
            dv[...] += dot(eb, g, NN)
            dk[...] += dot(ds, qn, NN)
            dq = dot(kt[...], ds, NN).T * SCALE
            rout[rows, 1, :, columns] = norm_back(q, gq, dq).reshape(BLOCK, ROWS, HS)
            return carry

        lax.fori_loop(0, SEQ // BLOCK, step, 0)
        rout[:, 2, :, columns] = norm_back(k_img, gk, dk[:L] * SCALE).reshape(SEQ, ROWS, HS)
        rout[:, 3, :, columns] = dv[:L].astype(jnp.bfloat16).reshape(SEQ, ROWS, HS)
        d_txt[:, 0, columns] = norm_back(txt[:, 0, columns].astype(jnp.float32), gt, dk[L:] * SCALE)
        d_txt[:, 1, columns] = jnp.where(live, dv[L:], 0.0).astype(jnp.bfloat16)
    copies = [pltpu.make_async_copy(rout.at[s], r, sems.at[s]) for s, r in enumerate(sent)]
    for copy in copies:
        copy.start()
    for copy in copies:
        copy.wait()


MESSAGE = jax.ShapeDtypeStruct((4, ROWS, WIDTH), jnp.bfloat16)
SMEM = pl.BlockSpec(memory_space=pltpu.SMEM)
VMEM = pl.BlockSpec(memory_space=pltpu.VMEM)
ANY = pl.BlockSpec(memory_space=pl.ANY)


def attend(length, txt, gate, gain_q, gain_k, gain_t, received):
    prompt = jax.ShapeDtypeStruct((PROMPT, 2, WIDTH), jnp.bfloat16)
    results = pl.pallas_call(
        attend_kernel,
        out_shape=[MESSAGE] * SEQ + [prompt],
        in_specs=[SMEM] + [VMEM] * 5 + [ANY] * SEQ,
        out_specs=[ANY] * SEQ + [VMEM],
        scratch_shapes=[
            pltpu.VMEM((SEQ, 4, ROWS, WIDTH), jnp.bfloat16),
            pltpu.VMEM((SEQ, 4, ROWS, WIDTH), jnp.bfloat16),
            pltpu.VMEM((KEYS, HS), jnp.bfloat16),
            pltpu.VMEM((HS, KEYS), jnp.bfloat16),
            pltpu.VMEM((KEYS, 2 * HS), jnp.bfloat16),
            pltpu.VMEM((2 * HS, KEYS), jnp.bfloat16),
            pltpu.VMEM((KEYS, HS), jnp.float32),
            pltpu.VMEM((KEYS, HS), jnp.float32),
            pltpu.SemaphoreType.DMA((SEQ,)),
        ],
        compiler_params=pltpu.CompilerParams(vmem_limit_bytes=32 * 1024 * 1024),
        name="attend",
    )(length, txt, gate, gain_q, gain_k, gain_t, *received)
    return results[:SEQ], results[SEQ]


def pack(place, img, cot):
    return pl.pallas_call(
        pack_kernel,
        out_shape=[MESSAGE] * SEQ,
        in_specs=[SMEM, VMEM, VMEM],
        out_specs=[VMEM] * SEQ,
        compiler_params=pltpu.CompilerParams(vmem_limit_bytes=16 * 1024 * 1024),
        name="pack",
    )(place, img, cot)


def unpack(place, packed):
    return pl.pallas_call(
        unpack_kernel,
        out_shape=(
            jax.ShapeDtypeStruct((ROWS, D), jnp.bfloat16),
            jax.ShapeDtypeStruct((3, ROWS, D), jnp.bfloat16),
        ),
        in_specs=[SMEM] + [VMEM] * SEQ,
        out_specs=(VMEM, VMEM),
        compiler_params=pltpu.CompilerParams(vmem_limit_bytes=16 * 1024 * 1024),
        name="unpack",
    )(place, *packed)


def exchange(parts, way):
    results = []
    for offset, part in zip(OFFSETS, parts):
        if offset != (0, 0):
            pairs = [(me, partner(me // 2, me % 2, offset)) for me in range(SEQ)]
            part = lax.ppermute(part, "seq", pairs if way == 1 else [(b, a) for a, b in pairs])
        results.append(part)
    return results


def local(img_qkv, txt_kv, cot_img, timesteps, lengths, gate_w, gain_q, gain_k, gain_t):
    samples, text_rows = txt_kv.shape[:2]
    groups = ("grp", "fsdp")
    place = jnp.stack(position())
    messages = pack(place, img_qkv[0].transpose(1, 0, 2), cot_img[0])
    txt_kv, *messages = lax.optimization_barrier((txt_kv, *messages))
    received = exchange(messages, 1)
    prompt = lax.all_to_all(txt_kv, groups, split_axis=0, concat_axis=0, tiled=True)
    prompt = prompt.reshape(samples * text_rows, 2, WIDTH)
    embedded = embedding(timesteps, gate_w.shape[0] // 2)
    gate = jnp.dot(embedded, gate_w.astype(jnp.float32), precision=lax.Precision.HIGHEST)
    sent, d_txt = attend(
        lengths, prompt, gate, gain_q[None], gain_k[None], gain_t[None], received
    )
    grad_prompt = d_txt.reshape(samples, text_rows, 2, WIDTH)
    d_txt = lax.all_to_all(grad_prompt, groups, split_axis=0, concat_axis=0, tiled=True)
    out, grads = unpack(place, exchange(sent, -1))
    return out[None], grads.transpose(1, 0, 2)[None], d_txt


def solution(mesh):
    in_specs = (
        P(("grp", "fsdp"), "seq", None, None),
        P(None, ("grp", "fsdp"), None, "seq"),
        P(("grp", "fsdp"), "seq", None),
        P(("grp", "fsdp")),
        P(("grp", "fsdp")),
        P(None, "seq"),
        P(),
        P(),
        P(),
    )
    out_specs = (
        P(("grp", "fsdp"), "seq", None),
        P(("grp", "fsdp"), "seq", None, None),
        P(None, ("grp", "fsdp"), None, "seq"),
    )
    return jax.shard_map(local, mesh=mesh, in_specs=in_specs, out_specs=out_specs, check_vma=False)
```

```python
import functools
import math

import jax
import jax.numpy as jnp
from jax import lax
from jax.experimental import pallas as pl
from jax.experimental.pallas import tpu as pltpu
from jax.sharding import PartitionSpec as P

D = 2048
HEADS = 16
HS = D // HEADS
EPS = 1e-06
SCALE = 1.0 / math.sqrt(HS)
EXP2_SCALE = SCALE * math.log2(math.e)
CHIPS = 4
SEQ = 2 * CHIPS
OFFSETS = ((2, 0), (2, 1), (1, 0), (3, 0), (1, 1), (3, 1), (0, 1), (0, 0))
ROWS = 128
WIDTH = 256
HPD = WIDTH // HS
L = SEQ * ROWS
PROMPT = 256
KEYS = L + PROMPT
IN_PARTS, OUT_PARTS = 1, 1
IN_WIDTH, OUT_WIDTH = WIDTH // IN_PARTS, WIDTH // OUT_PARTS


def embedding(stamps, half_freq):
    frequency = jnp.exp(-math.log(10000.0) * jnp.arange(half_freq, dtype=jnp.float32) / half_freq)
    angles = stamps.astype(jnp.float32)[..., None] * frequency
    return jnp.concatenate([jnp.cos(angles), jnp.sin(angles)], axis=-1)


def normed(x, gain):
    r = lax.rsqrt(jnp.mean(x * x, axis=-1, keepdims=True) + EPS)
    return (x * r * gain).astype(jnp.bfloat16)


def norm_back(x, gain, upstream):
    r = lax.rsqrt(jnp.mean(x * x, axis=-1, keepdims=True) + EPS)
    weighted = upstream * gain
    along = jnp.mean(x * weighted, axis=-1, keepdims=True)
    return (weighted * r - x * (r * r * r * along)).astype(jnp.bfloat16)


def dot(a, b, dims):
    return lax.dot_general(a, b, (dims, ((), ())), preferred_element_type=jnp.float32)


NT = ((1,), (1,))
NN = ((1,), (0,))


def position():
    me = lax.axis_index("seq")
    return me // 2, me % 2


def partner(i, c, offset):
    dz, dc = offset
    return ((i + dz) % CHIPS) * 2 + (c + dc) % 2


def pack_kernel(place, img, cot, *outs):
    for h in range(IN_PARTS):
        for k, offset in enumerate(OFFSETS):
            out = outs[h * SEQ + k]
            d = partner(place[0], place[1], offset)
            columns = pl.ds(pl.multiple_of(d * WIDTH + h * IN_WIDTH, IN_WIDTH), IN_WIDTH)
            out[:3] = img[:, :, columns]
            out[3] = cot[:, columns]


def unpack_kernel(place, *refs):
    packed, (out, grads) = refs[:-2], refs[-2:]
    for h in range(OUT_PARTS):
        for k, offset in enumerate(OFFSETS):
            part = packed[h * SEQ + k]
            d = partner(place[0], place[1], offset)
            columns = pl.ds(pl.multiple_of(d * WIDTH + h * OUT_WIDTH, OUT_WIDTH), OUT_WIDTH)
            out[:, columns] = part[0]
            grads[:, :, columns] = part[1:]


def split_kernel(txt, tk, tv):
    tk[...] = txt[:, 0, :]
    tv[...] = txt[:, 1, :]


def attend_kernel(first, count, length, tk_ref, tv_ref, gate, gain_q, gain_k, gain_t, *refs):
    received, sent, (dtk, dtv) = refs[:SEQ], refs[SEQ : 2 * SEQ], refs[2 * SEQ : 2 * SEQ + 2]
    rin, rout, sems = refs[2 * SEQ + 2 :]
    start = 0 if received[0].shape[-1] == count * HS else first * HS
    copies = [
        pltpu.make_async_copy(r.at[:, :, pl.ds(start, count * HS)], rin.at[s], sems.at[s])
        for s, r in enumerate(received)
    ]
    for copy in copies:
        copy.start()
    for copy in copies:
        copy.wait()
    gq, gk, gt = gain_q[...], gain_k[...], gain_t[...]
    live = lax.broadcasted_iota(jnp.int32, (PROMPT, HS), 0) < length[0]
    lane = lax.broadcasted_iota(jnp.int32, (L, HS), 1)
    for h in range(count):
        columns = pl.ds(h * HS, HS)
        there = pl.ds((first + h) * HS, HS)
        gate_h = gate[:, there]
        q = rin[:, 0, :, columns].reshape(L, HS).astype(jnp.float32)
        k = rin[:, 1, :, columns].reshape(L, HS).astype(jnp.float32)
        v = rin[:, 2, :, columns].reshape(L, HS)
        cot = rin[:, 3, :, columns].reshape(L, HS).astype(jnp.float32)
        tk = tk_ref[:, there].astype(jnp.float32)
        tv = jnp.where(live, tv_ref[:, there].astype(jnp.float32), 0.0).astype(jnp.bfloat16)
        qn = normed(q, gq)
        kn = jnp.concatenate([normed(k, gk), normed(tk, gt)], axis=0)
        ones = jnp.concatenate(
            [jnp.ones((L, HS), jnp.bfloat16), jnp.where(live, 1.0, 0.0).astype(jnp.bfloat16)], axis=0
        )
        ve = jnp.concatenate([jnp.concatenate([v, tv], axis=0), ones], axis=1)
        e = jnp.exp2(dot(kn, qn, NT) * EXP2_SCALE)
        eb = e.astype(jnp.bfloat16)
        sums = dot(ve.T, eb, NN).T
        rz = 1.0 / sums[:, HS:]
        attn = sums[:, :HS] * rz
        rout[:, 0, :, columns] = (attn * gate_h).astype(jnp.bfloat16).reshape(SEQ, ROWS, HS)
        g = (cot * gate_h * rz).astype(jnp.bfloat16)
        delta = -jnp.sum(g.astype(jnp.float32) * attn, axis=-1, keepdims=True)
        hi = delta.astype(jnp.bfloat16).astype(jnp.float32)
        mid = (delta - hi).astype(jnp.bfloat16).astype(jnp.float32)
        low = delta - hi - mid
        tail = jnp.where(lane == 0, hi, jnp.where(lane == 1, mid, jnp.where(lane == 2, low, 0.0)))
        ge = jnp.concatenate([g, tail.astype(jnp.bfloat16)], axis=1)
        ds = (e * dot(ve, ge, NT)).astype(jnp.bfloat16)
        dv = dot(eb, g, NN)
        rout[:, 3, :, columns] = dv[:L].astype(jnp.bfloat16).reshape(SEQ, ROWS, HS)
        dtv[:, columns] = jnp.where(live, dv[L:], 0.0).astype(jnp.bfloat16)
        dk = dot(ds, qn, NN) * SCALE
        rout[:, 2, :, columns] = norm_back(k, gk, dk[:L]).reshape(SEQ, ROWS, HS)
        dtk[:, columns] = norm_back(tk, gt, dk[L:])
        dq = dot(kn.T, ds, NN).T * SCALE
        rout[:, 1, :, columns] = norm_back(q, gq, dq).reshape(SEQ, ROWS, HS)
    copies = [pltpu.make_async_copy(rout.at[s], r, sems.at[s]) for s, r in enumerate(sent)]
    for copy in copies:
        copy.start()
    for copy in copies:
        copy.wait()


def message(width):
    return jax.ShapeDtypeStruct((4, ROWS, width), jnp.bfloat16)


SMEM = pl.BlockSpec(memory_space=pltpu.SMEM)
VMEM = pl.BlockSpec(memory_space=pltpu.VMEM)
ANY = pl.BlockSpec(memory_space=pl.ANY)


def attend(first, count, length, tk, tv, gate, gain_q, gain_k, gain_t, received):
    width = count * HS
    prompt = jax.ShapeDtypeStruct((PROMPT, width), jnp.bfloat16)
    results = pl.pallas_call(
        functools.partial(attend_kernel, first, count),
        out_shape=[message(width)] * SEQ + [prompt] * 2,
        in_specs=[SMEM] + [VMEM] * 6 + [ANY] * SEQ,
        out_specs=[ANY] * SEQ + [VMEM] * 2,
        scratch_shapes=[
            pltpu.VMEM((SEQ, 4, ROWS, width), jnp.bfloat16),
            pltpu.VMEM((SEQ, 4, ROWS, width), jnp.bfloat16),
            pltpu.SemaphoreType.DMA((SEQ,)),
        ],
        compiler_params=pltpu.CompilerParams(vmem_limit_bytes=44 * 1024 * 1024),
        cost_estimate=pl.CostEstimate(
            flops=count * 12 * L * KEYS * HS, bytes_accessed=count * 4 * 1024 * 1024, transcendentals=count * L * KEYS
        ),
        name="attend",
    )(length, tk, tv, gate, gain_q, gain_k, gain_t, *received)
    return results[:SEQ], results[SEQ], results[SEQ + 1]


def pack(place, img, cot):
    return pl.pallas_call(
        pack_kernel,
        out_shape=[message(IN_WIDTH)] * (SEQ * IN_PARTS),
        in_specs=[SMEM, VMEM, VMEM],
        out_specs=[VMEM] * (SEQ * IN_PARTS),
        compiler_params=pltpu.CompilerParams(vmem_limit_bytes=16 * 1024 * 1024),
        name="pack",
    )(place, img, cot)


def split(txt):
    return pl.pallas_call(
        split_kernel,
        out_shape=[jax.ShapeDtypeStruct((PROMPT, WIDTH), jnp.bfloat16)] * 2,
        in_specs=[VMEM],
        out_specs=[VMEM] * 2,
        compiler_params=pltpu.CompilerParams(vmem_limit_bytes=8 * 1024 * 1024),
        name="split",
    )(txt)


def unpack(place, packed):
    return pl.pallas_call(
        unpack_kernel,
        out_shape=(
            jax.ShapeDtypeStruct((ROWS, D), jnp.bfloat16),
            jax.ShapeDtypeStruct((3, ROWS, D), jnp.bfloat16),
        ),
        in_specs=[SMEM] + [VMEM] * (SEQ * OUT_PARTS),
        out_specs=(VMEM, VMEM),
        compiler_params=pltpu.CompilerParams(vmem_limit_bytes=16 * 1024 * 1024),
        name="unpack",
    )(place, *packed)


def exchange(parts, way):
    results = []
    for offset, part in zip(OFFSETS * (len(parts) // SEQ), parts):
        if offset != (0, 0):
            pairs = [(me, partner(me // 2, me % 2, offset)) for me in range(SEQ)]
            part = lax.ppermute(part, "seq", pairs if way == 1 else [(b, a) for a, b in pairs])
        results.append(part)
    return results


def local(img_qkv, txt_kv, cot_img, timesteps, lengths, gate_w, gain_q, gain_k, gain_t):
    samples, text_rows = txt_kv.shape[:2]
    groups = ("grp", "fsdp")
    place = jnp.stack(position())
    messages = pack(place, img_qkv[0].transpose(1, 0, 2), cot_img[0])
    txt_kv, *messages = lax.optimization_barrier((txt_kv, *messages))
    received = exchange(messages, 1)
    prompt = lax.all_to_all(txt_kv, groups, split_axis=0, concat_axis=0, tiled=True)
    tk, tv = split(prompt.reshape(samples * text_rows, 2, WIDTH))
    embedded = embedding(timesteps, gate_w.shape[0] // 2)
    gate = jnp.dot(embedded, gate_w.astype(jnp.float32), precision=lax.Precision.HIGHEST)
    returned, d_prompt = [], []
    count = HPD // OUT_PARTS
    for p in range(OUT_PARTS):
        part = received[p * SEQ : (p + 1) * SEQ] if IN_PARTS > 1 else received
        sent, dtk, dtv = attend(
            p * count, count, lengths, tk, tv, gate, gain_q[None], gain_k[None], gain_t[None], part
        )
        returned += exchange(sent, -1)
        d_prompt.append(jnp.stack([dtk, dtv], axis=1))
    d_txt = jnp.concatenate(d_prompt, axis=-1).reshape(samples, text_rows, 2, WIDTH)
    d_txt = lax.all_to_all(d_txt, groups, split_axis=0, concat_axis=0, tiled=True)
    out, grads = unpack(place, returned)
    return out[None], grads.transpose(1, 0, 2)[None], d_txt


def solution(mesh):
    in_specs = (
        P(("grp", "fsdp"), "seq", None, None),
        P(None, ("grp", "fsdp"), None, "seq"),
        P(("grp", "fsdp"), "seq", None),
        P(("grp", "fsdp")),
        P(("grp", "fsdp")),
        P(None, "seq"),
        P(),
        P(),
        P(),
    )
    out_specs = (
        P(("grp", "fsdp"), "seq", None),
        P(("grp", "fsdp"), "seq", None, None),
        P(None, ("grp", "fsdp"), None, "seq"),
    )
    return jax.shard_map(local, mesh=mesh, in_specs=in_specs, out_specs=out_specs, check_vma=False)
```

```python
import functools
import math

import jax
import jax.numpy as jnp
from jax import lax
from jax.experimental import pallas as pl
from jax.experimental.pallas import tpu as pltpu
from jax.sharding import PartitionSpec as P

D = 2048
HEADS = 16
HS = D // HEADS
EPS = 1e-06
SCALE = 1.0 / math.sqrt(HS)
EXP2_SCALE = SCALE * math.log2(math.e)
CHIPS = 4
SEQ = 2 * CHIPS
OFFSETS = ((2, 0), (2, 1), (1, 0), (3, 0), (1, 1), (3, 1), (0, 1), (0, 0))
ROWS = 128
WIDTH = 256
HPD = WIDTH // HS
L = SEQ * ROWS
PROMPT = 256
KEYS = L + PROMPT
IN_PARTS, OUT_PARTS = 1, 1
IN_WIDTH, OUT_WIDTH = WIDTH // IN_PARTS, WIDTH // OUT_PARTS


def embedding(stamps, half_freq):
    frequency = jnp.exp(-math.log(10000.0) * jnp.arange(half_freq, dtype=jnp.float32) / half_freq)
    angles = stamps.astype(jnp.float32)[..., None] * frequency
    return jnp.concatenate([jnp.cos(angles), jnp.sin(angles)], axis=-1)


def normed(x, gain):
    r = lax.rsqrt(jnp.mean(x * x, axis=-1, keepdims=True) + EPS)
    return (x * r * gain).astype(jnp.bfloat16)


def norm_back(x, gain, upstream):
    r = lax.rsqrt(jnp.mean(x * x, axis=-1, keepdims=True) + EPS)
    weighted = upstream * gain
    along = jnp.mean(x * weighted, axis=-1, keepdims=True)
    return (weighted * r - x * (r * r * r * along)).astype(jnp.bfloat16)


def dot(a, b, dims):
    return lax.dot_general(a, b, (dims, ((), ())), preferred_element_type=jnp.float32)


NT = ((1,), (1,))
NN = ((1,), (0,))


def position():
    me = lax.axis_index("seq")
    return me // 2, me % 2


def partner(i, c, offset):
    dz, dc = offset
    return ((i + dz) % CHIPS) * 2 + (c + dc) % 2


def pack_kernel(place, img, cot, *outs):
    for h in range(IN_PARTS):
        for k, offset in enumerate(OFFSETS):
            out = outs[h * SEQ + k]
            d = partner(place[0], place[1], offset)
            columns = pl.ds(pl.multiple_of(d * WIDTH + h * IN_WIDTH, IN_WIDTH), IN_WIDTH)
            out[:3] = img[:, :, columns]
            out[3] = cot[:, columns]


def unpack_kernel(place, *refs):
    packed, (out, grads) = refs[:-2], refs[-2:]
    for h in range(OUT_PARTS):
        for k, offset in enumerate(OFFSETS):
            part = packed[h * SEQ + k]
            d = partner(place[0], place[1], offset)
            columns = pl.ds(pl.multiple_of(d * WIDTH + h * OUT_WIDTH, OUT_WIDTH), OUT_WIDTH)
            out[:, columns] = part[0]
            grads[:, :, columns] = part[1:]


def split_kernel(txt, tk, tv):
    tk[...] = txt[:, 0, :]
    tv[...] = txt[:, 1, :]


def merge_kernel(dtk, dtv, d_txt):
    d_txt[:, 0, :] = dtk[...]
    d_txt[:, 1, :] = dtv[...]


def attend_kernel(first, count, length, tk_ref, tv_ref, gate, gain_q, gain_k, gain_t, *refs):
    received, sent, (dtk, dtv) = refs[:SEQ], refs[SEQ : 2 * SEQ], refs[2 * SEQ :]
    start = 0 if received[0].shape[-1] == count * HS else first * HS
    gq, gk, gt = gain_q[...], gain_k[...], gain_t[...]
    live = lax.broadcasted_iota(jnp.int32, (PROMPT, HS), 0) < length[0]
    lane = lax.broadcasted_iota(jnp.int32, (L, HS), 1)

    def gather(a, h):
        return jnp.concatenate([r[a, :, pl.ds(start + h * HS, HS)] for r in received], axis=0)

    def scatter(a, h, values):
        for s, r in enumerate(sent):
            r[a, :, pl.ds(h * HS, HS)] = values[s * ROWS : (s + 1) * ROWS]

    def head(h):
        columns = pl.ds(h * HS, HS)
        there = pl.ds((first + h) * HS, HS)
        gate_h = gate[:, there]
        q = gather(0, h).astype(jnp.float32)
        k = gather(1, h).astype(jnp.float32)
        v = gather(2, h)
        cot = gather(3, h).astype(jnp.float32)
        tk = tk_ref[:, there].astype(jnp.float32)
        tv = jnp.where(live, tv_ref[:, there].astype(jnp.float32), 0.0).astype(jnp.bfloat16)
        qn = normed(q, gq)
        kn = jnp.concatenate([normed(k, gk), normed(tk, gt)], axis=0)
        ones = jnp.concatenate(
            [jnp.ones((L, HS), jnp.bfloat16), jnp.where(live, 1.0, 0.0).astype(jnp.bfloat16)], axis=0
        )
        ve = jnp.concatenate([jnp.concatenate([v, tv], axis=0), ones], axis=1)
        e = jnp.exp2(dot(kn, qn, NT) * EXP2_SCALE)
        eb = e.astype(jnp.bfloat16)
        yield
        sums = dot(ve.T, eb, NN).T
        yield
        rz = 1.0 / sums[:, HS:]
        attn = sums[:, :HS] * rz
        scatter(0, h, (attn * gate_h).astype(jnp.bfloat16))
        g = (cot * gate_h * rz).astype(jnp.bfloat16)
        delta = -jnp.sum(g.astype(jnp.float32) * attn, axis=-1, keepdims=True)
        hi = delta.astype(jnp.bfloat16).astype(jnp.float32)
        mid = (delta - hi).astype(jnp.bfloat16).astype(jnp.float32)
        low = delta - hi - mid
        tail = jnp.where(lane == 0, hi, jnp.where(lane == 1, mid, jnp.where(lane == 2, low, 0.0)))
        ge = jnp.concatenate([g, tail.astype(jnp.bfloat16)], axis=1)
        yield
        ds = (e * dot(ve, ge, NT)).astype(jnp.bfloat16)
        yield
        dv = dot(eb, g, NN)
        yield
        scatter(3, h, dv[:L].astype(jnp.bfloat16))
        dtv[:, columns] = jnp.where(live, dv[L:], 0.0).astype(jnp.bfloat16)
        dk = dot(ds, qn, NN) * SCALE
        yield
        scatter(2, h, norm_back(k, gk, dk[:L]))
        dtk[:, columns] = norm_back(tk, gt, dk[L:])
        dq = dot(kn.T, ds, NN).T * SCALE
        scatter(1, h, norm_back(q, gq, dq))
        yield

    heads = [head(h) for h in range(count)]
    next(heads[0])
    while heads:
        heads = [g for g in heads if next(g, heads) is not heads]


def message(width):
    return jax.ShapeDtypeStruct((4, ROWS, width), jnp.bfloat16)


SMEM = pl.BlockSpec(memory_space=pltpu.SMEM)
VMEM = pl.BlockSpec(memory_space=pltpu.VMEM)
ANY = pl.BlockSpec(memory_space=pl.ANY)


def attend(first, count, length, tk, tv, gate, gain_q, gain_k, gain_t, received):
    width = count * HS
    prompt = jax.ShapeDtypeStruct((PROMPT, width), jnp.bfloat16)
    results = pl.pallas_call(
        functools.partial(attend_kernel, first, count),
        out_shape=[message(width)] * SEQ + [prompt] * 2,
        in_specs=[SMEM] + [VMEM] * (6 + SEQ),
        out_specs=[VMEM] * (SEQ + 2),
        compiler_params=pltpu.CompilerParams(vmem_limit_bytes=44 * 1024 * 1024),
        cost_estimate=pl.CostEstimate(
            flops=count * 12 * L * KEYS * HS, bytes_accessed=count * 4 * 1024 * 1024, transcendentals=count * L * KEYS
        ),
        name="attend",
    )(length, tk, tv, gate, gain_q, gain_k, gain_t, *received)
    return results[:SEQ], results[SEQ], results[SEQ + 1]


def pack(place, img, cot):
    return pl.pallas_call(
        pack_kernel,
        out_shape=[message(IN_WIDTH)] * (SEQ * IN_PARTS),
        in_specs=[SMEM, VMEM, VMEM],
        out_specs=[VMEM] * (SEQ * IN_PARTS),
        compiler_params=pltpu.CompilerParams(vmem_limit_bytes=16 * 1024 * 1024),
        name="pack",
    )(place, img, cot)


def split(txt):
    return pl.pallas_call(
        split_kernel,
        out_shape=[jax.ShapeDtypeStruct((PROMPT, WIDTH), jnp.bfloat16)] * 2,
        in_specs=[VMEM],
        out_specs=[VMEM] * 2,
        compiler_params=pltpu.CompilerParams(vmem_limit_bytes=8 * 1024 * 1024),
        name="split",
    )(txt)


def merge(dtk, dtv):
    return pl.pallas_call(
        merge_kernel,
        out_shape=jax.ShapeDtypeStruct((PROMPT, 2, WIDTH), jnp.bfloat16),
        in_specs=[VMEM] * 2,
        out_specs=VMEM,
        compiler_params=pltpu.CompilerParams(vmem_limit_bytes=8 * 1024 * 1024),
        name="merge",
    )(dtk, dtv)


def unpack(place, packed):
    return pl.pallas_call(
        unpack_kernel,
        out_shape=(
            jax.ShapeDtypeStruct((ROWS, D), jnp.bfloat16),
            jax.ShapeDtypeStruct((3, ROWS, D), jnp.bfloat16),
        ),
        in_specs=[SMEM] + [VMEM] * (SEQ * OUT_PARTS),
        out_specs=(VMEM, VMEM),
        compiler_params=pltpu.CompilerParams(vmem_limit_bytes=16 * 1024 * 1024),
        name="unpack",
    )(place, *packed)


def exchange(parts, way):
    results = []
    for offset, part in zip(OFFSETS * (len(parts) // SEQ), parts):
        if offset != (0, 0):
            pairs = [(me, partner(me // 2, me % 2, offset)) for me in range(SEQ)]
            part = lax.ppermute(part, "seq", pairs if way == 1 else [(b, a) for a, b in pairs])
        results.append(part)
    return results


def local(img_qkv, txt_kv, cot_img, timesteps, lengths, gate_w, gain_q, gain_k, gain_t):
    samples, text_rows = txt_kv.shape[:2]
    groups = ("grp", "fsdp")
    place = jnp.stack(position())
    messages = pack(place, img_qkv[0].transpose(1, 0, 2), cot_img[0])
    txt_kv, *messages = lax.optimization_barrier((txt_kv, *messages))
    received = exchange(messages, 1)
    prompt = lax.all_to_all(txt_kv, groups, split_axis=0, concat_axis=0, tiled=True)
    tk, tv = split(prompt.reshape(samples * text_rows, 2, WIDTH))
    embedded = embedding(timesteps, gate_w.shape[0] // 2)
    gate = jnp.dot(embedded, gate_w.astype(jnp.float32), precision=lax.Precision.HIGHEST)
    returned, d_prompt = [], []
    count = HPD // OUT_PARTS
    for p in range(OUT_PARTS):
        part = received[p * SEQ : (p + 1) * SEQ] if IN_PARTS > 1 else received
        sent, dtk, dtv = attend(
            p * count, count, lengths, tk, tv, gate, gain_q[None], gain_k[None], gain_t[None], part
        )
        returned += exchange(sent, -1)
        d_prompt.append(merge(dtk, dtv))
    d_txt = jnp.concatenate(d_prompt, axis=-1).reshape(samples, text_rows, 2, WIDTH)
    d_txt = lax.all_to_all(d_txt, groups, split_axis=0, concat_axis=0, tiled=True)
    out, grads = unpack(place, returned)
    return out[None], grads.transpose(1, 0, 2)[None], d_txt


def solution(mesh):
    in_specs = (
        P(("grp", "fsdp"), "seq", None, None),
        P(None, ("grp", "fsdp"), None, "seq"),
        P(("grp", "fsdp"), "seq", None),
        P(("grp", "fsdp")),
        P(("grp", "fsdp")),
        P(None, "seq"),
        P(),
        P(),
        P(),
    )
    out_specs = (
        P(("grp", "fsdp"), "seq", None),
        P(("grp", "fsdp"), "seq", None, None),
        P(None, ("grp", "fsdp"), None, "seq"),
    )
    return jax.shard_map(local, mesh=mesh, in_specs=in_specs, out_specs=out_specs, check_vma=False)
```

```python
import functools
import math

import jax
import jax.numpy as jnp
from jax import lax
from jax.experimental import pallas as pl
from jax.experimental.pallas import tpu as pltpu
from jax.sharding import PartitionSpec as P

D = 2048
HEADS = 16
HS = D // HEADS
EPS = 1e-06
SCALE = 1.0 / math.sqrt(HS)
EXP2_SCALE = SCALE * math.log2(math.e)
CHIPS = 4
SEQ = 2 * CHIPS
OFFSETS = ((2, 0), (2, 1), (1, 0), (3, 0), (1, 1), (3, 1), (0, 1), (0, 0))
ROWS = 128
WIDTH = 256
HPD = WIDTH // HS
L = SEQ * ROWS
PROMPT = 256
KEYS = L + PROMPT
IN_PARTS, OUT_PARTS = 1, 1
IN_WIDTH, OUT_WIDTH = WIDTH // IN_PARTS, WIDTH // OUT_PARTS


def embedding(stamps, half_freq):
    frequency = jnp.exp(-math.log(10000.0) * jnp.arange(half_freq, dtype=jnp.float32) / half_freq)
    angles = stamps.astype(jnp.float32)[..., None] * frequency
    return jnp.concatenate([jnp.cos(angles), jnp.sin(angles)], axis=-1)


def normed(x, gain):
    r = lax.rsqrt(jnp.mean(x * x, axis=-1, keepdims=True) + EPS)
    return (x * r * gain).astype(jnp.bfloat16)


def norm_back(x, gain, upstream):
    r = lax.rsqrt(jnp.mean(x * x, axis=-1, keepdims=True) + EPS)
    weighted = upstream * gain
    along = jnp.mean(x * weighted, axis=-1, keepdims=True)
    return (weighted * r - x * (r * r * r * along)).astype(jnp.bfloat16)


def dot(a, b, dims):
    return lax.dot_general(a, b, (dims, ((), ())), preferred_element_type=jnp.float32)


NT = ((1,), (1,))
NN = ((1,), (0,))


def position():
    me = lax.axis_index("seq")
    return me // 2, me % 2


def partner(i, c, offset):
    dz, dc = offset
    return ((i + dz) % CHIPS) * 2 + (c + dc) % 2


def pack_kernel(place, img, cot, *outs):
    for h in range(IN_PARTS):
        for k, offset in enumerate(OFFSETS):
            out = outs[h * SEQ + k]
            d = partner(place[0], place[1], offset)
            columns = pl.ds(pl.multiple_of(d * WIDTH + h * IN_WIDTH, IN_WIDTH), IN_WIDTH)
            out[:3] = img[:, :, columns]
            out[3] = cot[:, columns]


def unpack_kernel(place, d_txt, *refs):
    packed, (out, grads, prompt_out, sems) = refs[:SEQ], refs[SEQ:]
    copies = [pltpu.make_async_copy(d_txt, prompt_out, sems.at[SEQ, 0])]
    for k, offset in enumerate(OFFSETS):
        d = partner(place[0], place[1], offset)
        columns = pl.ds(pl.multiple_of(d * WIDTH, WIDTH), WIDTH)
        copies.append(pltpu.make_async_copy(packed[k].at[0], out.at[:, columns], sems.at[k, 0]))
        copies.append(pltpu.make_async_copy(packed[k].at[pl.ds(1, 3)], grads.at[:, :, columns], sems.at[k, 1]))
    for copy in copies:
        copy.start()
    for copy in copies:
        copy.wait()


def split_kernel(txt, tk, tv):
    tk[...] = txt[:, 0, :]
    tv[...] = txt[:, 1, :]


def merge_kernel(dtk, dtv, d_txt):
    d_txt[:, 0, :] = dtk[...]
    d_txt[:, 1, :] = dtv[...]


def attend_kernel(first, count, length, tk_ref, tv_ref, gate, gain_q, gain_k, gain_t, *refs):
    received, sent, (dtk, dtv) = refs[:SEQ], refs[SEQ : 2 * SEQ], refs[2 * SEQ :]
    start = 0 if received[0].shape[-1] == count * HS else first * HS
    gq, gk, gt = gain_q[...], gain_k[...], gain_t[...]
    live = lax.broadcasted_iota(jnp.int32, (PROMPT, HS), 0) < length[0]
    lane = lax.broadcasted_iota(jnp.int32, (L, HS), 1)

    def gather(a, h):
        return jnp.concatenate([r[a, :, pl.ds(start + h * HS, HS)] for r in received], axis=0)

    def scatter(a, h, values):
        for s, r in enumerate(sent):
            r[a, :, pl.ds(h * HS, HS)] = values[s * ROWS : (s + 1) * ROWS]

    def head(h):
        columns = pl.ds(h * HS, HS)
        there = pl.ds((first + h) * HS, HS)
        gate_h = gate[:, there]
        q = gather(0, h).astype(jnp.float32)
        k = gather(1, h).astype(jnp.float32)
        v = gather(2, h)
        cot = gather(3, h).astype(jnp.float32)
        tk = tk_ref[:, there].astype(jnp.float32)
        tv = jnp.where(live, tv_ref[:, there].astype(jnp.float32), 0.0).astype(jnp.bfloat16)
        qn = normed(q, gq)
        kn = jnp.concatenate([normed(k, gk), normed(tk, gt)], axis=0)
        ones = jnp.concatenate(
            [jnp.ones((L, HS), jnp.bfloat16), jnp.where(live, 1.0, 0.0).astype(jnp.bfloat16)], axis=0
        )
        ve = jnp.concatenate([jnp.concatenate([v, tv], axis=0), ones], axis=1)
        e = jnp.exp2(dot(kn, qn, NT) * EXP2_SCALE)
        eb = e.astype(jnp.bfloat16)
        yield
        sums = dot(ve.T, eb, NN).T
        yield
        rz = 1.0 / sums[:, HS:]
        attn = sums[:, :HS] * rz
        scatter(0, h, (attn * gate_h).astype(jnp.bfloat16))
        g = (cot * gate_h * rz).astype(jnp.bfloat16)
        delta = -jnp.sum(g.astype(jnp.float32) * attn, axis=-1, keepdims=True)
        hi = delta.astype(jnp.bfloat16).astype(jnp.float32)
        mid = (delta - hi).astype(jnp.bfloat16).astype(jnp.float32)
        low = delta - hi - mid
        tail = jnp.where(lane == 0, hi, jnp.where(lane == 1, mid, jnp.where(lane == 2, low, 0.0)))
        ge = jnp.concatenate([g, tail.astype(jnp.bfloat16)], axis=1)
        yield
        ds = (e * dot(ve, ge, NT)).astype(jnp.bfloat16)
        yield
        dv = dot(eb, g, NN)
        yield
        scatter(3, h, dv[:L].astype(jnp.bfloat16))
        dtv[:, columns] = jnp.where(live, dv[L:], 0.0).astype(jnp.bfloat16)
        dk = dot(ds, qn, NN) * SCALE
        yield
        scatter(2, h, norm_back(k, gk, dk[:L]))
        dtk[:, columns] = norm_back(tk, gt, dk[L:])
        dq = dot(kn.T, ds, NN).T * SCALE
        scatter(1, h, norm_back(q, gq, dq))
        yield

    heads = [head(h) for h in range(count)]
    next(heads[0])
    while heads:
        heads = [g for g in heads if next(g, heads) is not heads]


def message(width):
    return jax.ShapeDtypeStruct((4, ROWS, width), jnp.bfloat16)


SMEM = pl.BlockSpec(memory_space=pltpu.SMEM)
VMEM = pl.BlockSpec(memory_space=pltpu.VMEM)
ANY = pl.BlockSpec(memory_space=pl.ANY)


def attend(first, count, length, tk, tv, gate, gain_q, gain_k, gain_t, received):
    width = count * HS
    prompt = jax.ShapeDtypeStruct((PROMPT, width), jnp.bfloat16)
    results = pl.pallas_call(
        functools.partial(attend_kernel, first, count),
        out_shape=[message(width)] * SEQ + [prompt] * 2,
        in_specs=[SMEM] + [VMEM] * (6 + SEQ),
        out_specs=[VMEM] * (SEQ + 2),
        compiler_params=pltpu.CompilerParams(vmem_limit_bytes=44 * 1024 * 1024),
        cost_estimate=pl.CostEstimate(
            flops=count * 12 * L * KEYS * HS, bytes_accessed=count * 4 * 1024 * 1024, transcendentals=count * L * KEYS
        ),
        name="attend",
    )(length, tk, tv, gate, gain_q, gain_k, gain_t, *received)
    return results[:SEQ], results[SEQ], results[SEQ + 1]


def pack(place, img, cot):
    return pl.pallas_call(
        pack_kernel,
        out_shape=[message(IN_WIDTH)] * (SEQ * IN_PARTS),
        in_specs=[SMEM, VMEM, VMEM],
        out_specs=[VMEM] * (SEQ * IN_PARTS),
        compiler_params=pltpu.CompilerParams(vmem_limit_bytes=16 * 1024 * 1024),
        name="pack",
    )(place, img, cot)


def split(txt):
    return pl.pallas_call(
        split_kernel,
        out_shape=[jax.ShapeDtypeStruct((PROMPT, WIDTH), jnp.bfloat16)] * 2,
        in_specs=[VMEM],
        out_specs=[VMEM] * 2,
        compiler_params=pltpu.CompilerParams(vmem_limit_bytes=8 * 1024 * 1024),
        name="split",
    )(txt)


def merge(dtk, dtv):
    return pl.pallas_call(
        merge_kernel,
        out_shape=jax.ShapeDtypeStruct((PROMPT, 2, WIDTH), jnp.bfloat16),
        in_specs=[VMEM] * 2,
        out_specs=VMEM,
        compiler_params=pltpu.CompilerParams(vmem_limit_bytes=8 * 1024 * 1024),
        name="merge",
    )(dtk, dtv)


def unpack(place, d_txt, packed):
    return pl.pallas_call(
        unpack_kernel,
        out_shape=(
            jax.ShapeDtypeStruct((ROWS, D), jnp.bfloat16),
            jax.ShapeDtypeStruct((3, ROWS, D), jnp.bfloat16),
            jax.ShapeDtypeStruct(d_txt.shape, jnp.bfloat16),
        ),
        in_specs=[SMEM] + [ANY] * (1 + SEQ),
        out_specs=(ANY, ANY, ANY),
        scratch_shapes=[pltpu.SemaphoreType.DMA((SEQ + 1, 2))],
        compiler_params=pltpu.CompilerParams(vmem_limit_bytes=16 * 1024 * 1024),
        name="unpack",
    )(place, d_txt, *packed)


def exchange(parts, way):
    results = []
    for offset, part in zip(OFFSETS * (len(parts) // SEQ), parts):
        if offset != (0, 0):
            pairs = [(me, partner(me // 2, me % 2, offset)) for me in range(SEQ)]
            part = lax.ppermute(part, "seq", pairs if way == 1 else [(b, a) for a, b in pairs])
        results.append(part)
    return results


def local(img_qkv, txt_kv, cot_img, timesteps, lengths, gate_w, gain_q, gain_k, gain_t):
    samples, text_rows = txt_kv.shape[:2]
    groups = ("grp", "fsdp")
    place = jnp.stack(position())
    messages = pack(place, img_qkv[0].transpose(1, 0, 2), cot_img[0])
    txt_kv, *messages = lax.optimization_barrier((txt_kv, *messages))
    received = exchange(messages, 1)
    prompt = lax.all_to_all(txt_kv, groups, split_axis=0, concat_axis=0, tiled=True)
    tk, tv = split(prompt.reshape(samples * text_rows, 2, WIDTH))
    embedded = embedding(timesteps, gate_w.shape[0] // 2)
    gate = jnp.dot(embedded, gate_w.astype(jnp.float32), precision=lax.Precision.HIGHEST)
    returned, d_prompt = [], []
    count = HPD // OUT_PARTS
    for p in range(OUT_PARTS):
        part = received[p * SEQ : (p + 1) * SEQ] if IN_PARTS > 1 else received
        sent, dtk, dtv = attend(
            p * count, count, lengths, tk, tv, gate, gain_q[None], gain_k[None], gain_t[None], part
        )
        returned += exchange(sent, -1)
        d_prompt.append(merge(dtk, dtv))
    d_txt = jnp.concatenate(d_prompt, axis=-1).reshape(samples, text_rows, 2, WIDTH)
    d_txt = lax.all_to_all(d_txt, groups, split_axis=0, concat_axis=0, tiled=True)
    out, grads, d_txt = unpack(place, d_txt, returned)
    return out[None], grads.transpose(1, 0, 2)[None], d_txt


def solution(mesh):
    in_specs = (
        P(("grp", "fsdp"), "seq", None, None),
        P(None, ("grp", "fsdp"), None, "seq"),
        P(("grp", "fsdp"), "seq", None),
        P(("grp", "fsdp")),
        P(("grp", "fsdp")),
        P(None, "seq"),
        P(),
        P(),
        P(),
    )
    out_specs = (
        P(("grp", "fsdp"), "seq", None),
        P(("grp", "fsdp"), "seq", None, None),
        P(None, ("grp", "fsdp"), None, "seq"),
    )
    return jax.shard_map(local, mesh=mesh, in_specs=in_specs, out_specs=out_specs, check_vma=False)
```
